32 devices in a mesh: grp: 4 (over x, core), dp: 8 (over z, y).
Axes of the slice: x: 2, y: 2, z: 4, core: 2. Of those that a mesh axis runs over, the one named last changes fastest.
Arguments:
- photo_vectors_raw: bfloat16 [32768, 768], P(('grp', 'dp')), may hold values from -0.21875 to 0.21875
- sentence_vectors_raw: bfloat16 [32768, 768], P(('grp', 'dp')), may hold values from -0.21875 to 0.21875
- companion_index: int32 [32, 1024], P(('grp', 'dp')), may hold values from 0 to 1023, each once within a row
- exponent_of_sharpness: float32 [1], replicated, may hold values from 1 to 2.3
- affinity_offset: float32 [1], replicated, may hold values from -4 to -1
Outputs:
- image_grad: float32 [32768, 768], P(('grp', 'dp'))
- text_grad: float32 [32768, 768], P(('grp', 'dp'))
The draws below stay inside these ranges and needn't reach their ends.
Inputs may be any that keep to these rules, and one draw needn't show every extreme that they name: Each row of companion_index is a permutation of 0 to 1023.
All inputs are finite; a program needn't handle non-finite values.
Results may differ from the reference program's by a relative error of at most 0.0055.
Values may be sent and summed in bfloat16 or wider, within the bound.
A program may use at most 128 MiB of HBM per device.

```python
import jax
import jax.numpy as jnp
from jax import lax

D = 768
ROWS = 1024
SEGMENT_COUNT = 32
TOKENS = 32768


def steps_of(own_key, dims, shards, smallest, top_value):
    level = 1.0
    for position, blocks in shards:
        heights = jax.random.uniform(jax.random.fold_in(jax.random.fold_in(own_key, 6), position), (blocks,), jnp.float32, smallest / len(shards), top_value / len(shards))
        level = level * jnp.repeat(jnp.exp(heights), dims[position] // blocks).reshape((-1,) + (1,) * (len(dims) - 1 - position))
    return level


def scatter_about(stream_key, dims, deviation, limit, shards=(), kind=jnp.bfloat16):
    level = steps_of(stream_key, dims, shards, -0.22, 0.18) if shards else 1.0
    drawn = jax.random.normal(stream_key, dims, jnp.float32) * deviation * level
    return jnp.minimum(jnp.maximum(drawn, -limit), limit).astype(kind)


def setup_inputs(seed: int = 0) -> dict:
    key_list = jax.random.split(jax.random.key(seed), 6)
    return {
        "photo_vectors_raw": scatter_about(key_list[0], (TOKENS, D), D ** -0.5, 0.21875, ((0, 32),)),
        "sentence_vectors_raw": scatter_about(key_list[1], (TOKENS, D), D ** -0.5, 0.21875, ((0, 32),)),
        "companion_index": jax.vmap(lambda own: jax.random.permutation(own, ROWS))(jax.random.split(key_list[2], SEGMENT_COUNT)).reshape((SEGMENT_COUNT, ROWS)).astype(jnp.int32),
        "exponent_of_sharpness": jnp.clip(jax.random.uniform(key_list[3], (1,), jnp.float32, 1.0, 2.3), 1.0, 2.3),
        "affinity_offset": jnp.clip(jax.random.uniform(key_list[4], (1,), jnp.float32, -4.0, -1.0), -4.0, -1.0),
    }


def unit_rows(raw):
    values = raw.astype(jnp.float32)
    inverse_norm = lax.rsqrt(lax.optimization_barrier(jnp.sum(values * values, -1, keepdims=True)) + 1e-06)
    return (values * inverse_norm, inverse_norm)

def gradient_panel(picture_rows, caption_rows, matching_pairs, sharpness_factor, block_distance):
    score_matrix = sharpness_factor * jnp.dot(picture_rows, caption_rows.T, preferred_element_type=jnp.float32) + block_distance
    if matching_pairs is None:
        target_labels = -1.0
    else:
        target_labels = jnp.where(matching_pairs, 1.0, -1.0)
    return (sharpness_factor * -target_labels * jax.nn.sigmoid(-target_labels * score_matrix)).astype(jnp.bfloat16)

def unit_backward(grad, unit, inverse_norm):
    return inverse_norm * (grad - unit * lax.optimization_barrier(jnp.sum(unit * grad, -1, keepdims=True)))

def reference(photo_vectors_raw, sentence_vectors_raw, companion_index, exponent_of_sharpness, affinity_offset):
    sharpness_factor = jnp.exp(exponent_of_sharpness[0])
    block_distance = affinity_offset[0]
    image_unit, image_norm = unit_rows(photo_vectors_raw)
    text_unit, text_norm = unit_rows(sentence_vectors_raw)
    image_blocks = image_unit.astype(jnp.bfloat16).reshape(SEGMENT_COUNT, ROWS, D)
    text_blocks = text_unit.astype(jnp.bfloat16).reshape(SEGMENT_COUNT, ROWS, D)

    def per_block(items):
        picture_rows, caption_rows, preceding_block, following_block, pairing = items
        matching_pairs = pairing[:, None] == jnp.arange(ROWS, dtype=jnp.int32)[None, :]
        local_panel = gradient_panel(picture_rows, caption_rows, matching_pairs, sharpness_factor, block_distance)
        leftward_panel = gradient_panel(picture_rows, preceding_block, None, sharpness_factor, block_distance)
        rightward_panel = gradient_panel(picture_rows, following_block, None, sharpness_factor, block_distance)
        image_part = jnp.dot(local_panel, caption_rows, preferred_element_type=jnp.float32)
        image_part = image_part + jnp.dot(leftward_panel, preceding_block, preferred_element_type=jnp.float32)
        image_part = image_part + jnp.dot(rightward_panel, following_block, preferred_element_type=jnp.float32)
        text_own = jnp.dot(local_panel.T, picture_rows, preferred_element_type=jnp.float32)
        text_left = jnp.dot(leftward_panel.T, picture_rows, preferred_element_type=jnp.float32)
        text_right = jnp.dot(rightward_panel.T, picture_rows, preferred_element_type=jnp.float32)
        return (image_part, text_own, text_left, text_right)
    image_part, text_own, text_left, text_right = lax.map(per_block, (image_blocks, text_blocks, jnp.roll(text_blocks, 1, 0), jnp.roll(text_blocks, -1, 0), companion_index))
    text_part = text_own + jnp.roll(text_left, -1, 0) + jnp.roll(text_right, 1, 0)
    image_grad = unit_backward(image_part.reshape(TOKENS, D), image_unit, image_norm)
    text_grad = unit_backward(text_part.reshape(TOKENS, D), text_unit, text_norm)
    return (image_grad, text_grad)
```

```python
import functools

import jax
import jax.numpy as jnp
from jax import lax
from jax.experimental import pallas as pl
from jax.experimental.pallas import tpu as pltpu
from jax.sharding import PartitionSpec as P

LOG2E = 1.4426950408889634
CHUNK = 128
TILE = 512
AHEAD = 2
LAG = 2


def rows_at(index, size):
    return pl.ds(pl.multiple_of(index * size, size), size)


def weights(scores, scale, shift, top):
    return top / (1.0 + jnp.exp2(scale * scores + shift))


def dot_t(left, right):
    return lax.dot_general(left, right, (((1,), (1,)), ((), ())), preferred_element_type=jnp.float32)


def kernel(
    sizes, image_ref, text_ref, pair_ref, exponent_ref, offset_ref, image_out, text_out,
    unit, norm, near, far, send_sem, near_sem, pass_sem, far_sem,
):
    ring, inner, rows, chunk, tile = sizes
    steps = rows // chunk
    me = lax.axis_index("grp") * inner + lax.axis_index("dp")
    odd = lax.rem(me, 2)
    partner = me + 1 - 2 * odd
    onward = lax.rem(me + 2 - 4 * odd + ring, ring)
    behind = lax.rem(me - 2 + 4 * odd + ring, ring)

    def place(index):
        return (index // inner, lax.rem(index, inner))

    barrier = pltpu.get_barrier_semaphore()
    for other in (partner, onward, behind):
        pl.semaphore_signal(barrier, inc=1, device_id=place(other), device_id_type=pl.DeviceIdType.MESH)
    pl.semaphore_wait(barrier, 3)

    def own_copy(kind, j):
        return pltpu.make_async_remote_copy(
            src_ref=unit.at[kind, rows_at(j, chunk)],
            dst_ref=near.at[kind, rows_at(j, chunk)],
            send_sem=send_sem.at[kind, j],
            recv_sem=near_sem.at[kind, j],
            device_id=place(partner),
            device_id_type=pl.DeviceIdType.MESH,
        )

    def pass_copy(kind, j):
        return pltpu.make_async_remote_copy(
            src_ref=near.at[kind, rows_at(j, chunk)],
            dst_ref=far.at[kind, rows_at(j, chunk)],
            send_sem=pass_sem.at[kind, j],
            recv_sem=far_sem.at[kind, j],
            device_id=place(onward),
            device_id_type=pl.DeviceIdType.MESH,
        )

    raws = (text_ref, image_ref)
    outs = (text_out, image_out)

    @pl.loop(0, steps)
    def _(j):
        at = rows_at(j, chunk)
        for kind in range(2):
            values = raws[kind][at, :].astype(jnp.float32)
            inverse = lax.rsqrt(jnp.sum(values * values, -1, keepdims=True) + 1e-06)
            norm[kind, at, :] = inverse
            unit[kind, at, :] = (values * inverse).astype(jnp.bfloat16)
            outs[kind][at, :] = jnp.zeros_like(values)

            @pl.when(j < AHEAD)
            def _():
                own_copy(kind, j).start()

    top = jnp.exp(jnp.full((1, chunk), exponent_ref[0], jnp.float32))
    scale = top * -LOG2E
    shift = jnp.full((1, chunk), offset_ref[0], jnp.float32) * -LOG2E

    def spread(kind, block):
        out = outs[1 - kind]

        @pl.loop(0, rows // tile)
        def _(r):
            at = rows_at(r, tile)
            panel = weights(dot_t(unit[1 - kind, at, :], block), scale, shift, top)
            out[at, :] += jnp.dot(panel.astype(jnp.bfloat16), block, preferred_element_type=jnp.float32)

    def own_block(j):
        chunk_at = rows_at(j, chunk)
        block = unit[1, chunk_at, :]
        match = pair_ref[:, chunk_at]

        @pl.loop(0, rows // tile)
        def _(r):
            at = rows_at(r, tile)
            captions = unit[0, at, :]
            hit = match == lax.broadcasted_iota(jnp.int32, (tile, chunk), 0) + r * tile
            scores = dot_t(captions, block)
            power = scale * scores + shift
            panel = top / (1.0 + jnp.exp2(jnp.where(hit, -power, power)))
            panel = jnp.where(hit, -panel, panel).astype(jnp.bfloat16)
            text_out[at, :] += jnp.dot(panel, block, preferred_element_type=jnp.float32)
            image_out[chunk_at, :] += lax.dot_general(
                panel, captions, (((0,), (0,)), ((), ())), preferred_element_type=jnp.float32
            )

    @pl.loop(0, steps + LAG)
    def _(j):
        @pl.when(j < steps)
        def _():
            own_block(j)
            for kind in range(2):
                own_copy(kind, j).wait_recv()
                pass_copy(kind, j).start()

                @pl.when(j + AHEAD < steps)
                def _():
                    own_copy(kind, j + AHEAD).start()

            for kind in range(2):
                spread(kind, near[kind, rows_at(j, chunk), :])

        @pl.when(j >= LAG)
        def _():
            for kind in range(2):
                pass_copy(kind, j - LAG).wait_recv()
                spread(kind, far[kind, rows_at(j - LAG, chunk), :])

    @pl.loop(0, steps)
    def _(j):
        at = rows_at(j, chunk)
        for kind in range(2):
            inverse = norm[kind, at, :]
            values = raws[kind][at, :].astype(jnp.float32) * inverse
            grad = outs[kind][at, :]
            outs[kind][at, :] = inverse * (grad - values * jnp.sum(values * grad, -1, keepdims=True))
            own_copy(kind, j).wait_send()
            pass_copy(kind, j).wait_send()


def local(ring, inner, photo, sentence, companion, exponent, offset):
    rows, width = photo.shape
    steps = rows // CHUNK
    vmem = pl.BlockSpec(memory_space=pltpu.VMEM)
    smem = pl.BlockSpec(memory_space=pltpu.SMEM)
    grad = jax.ShapeDtypeStruct((rows, width), jnp.float32)
    return pl.pallas_call(
        functools.partial(kernel, (ring, inner, rows, CHUNK, TILE)),
        out_shape=(grad, grad),
        in_specs=[vmem, vmem, vmem, smem, smem],
        out_specs=(vmem, vmem),
        scratch_shapes=[
            pltpu.VMEM((2, rows, width), jnp.bfloat16),
            pltpu.VMEM((2, rows, 1), jnp.float32),
            pltpu.VMEM((2, rows, width), jnp.bfloat16),
            pltpu.VMEM((2, rows, width), jnp.bfloat16),
            pltpu.SemaphoreType.DMA((2, steps)),
            pltpu.SemaphoreType.DMA((2, steps)),
            pltpu.SemaphoreType.DMA((2, steps)),
            pltpu.SemaphoreType.DMA((2, steps)),
        ],
        compiler_params=pltpu.CompilerParams(
            collective_id=0, has_side_effects=True, vmem_limit_bytes=48 * 1024 * 1024
        ),
        cost_estimate=pl.CostEstimate(
            flops=22 * rows * rows * width, bytes_accessed=12 * rows * width, transcendentals=10 * rows * rows
        ),
    )(photo, sentence, companion, exponent, offset)


def solution(mesh):
    inner = mesh.shape["dp"]
    ring = mesh.shape["grp"] * inner
    placed = (P(("grp", "dp"), None), P(("grp", "dp"), None), P(("grp", "dp"), None), P(), P())
    return jax.shard_map(
        functools.partial(local, ring, inner),
        mesh=mesh,
        in_specs=placed,
        out_specs=(P(("grp", "dp"), None), P(("grp", "dp"), None)),
        check_vma=False,
    )
```

```python
import functools

import jax
import jax.numpy as jnp
from jax import lax
from jax.experimental import pallas as pl
from jax.experimental.pallas import tpu as pltpu
from jax.sharding import PartitionSpec as P

LOG2E = 1.4426950408889634
SUB = 128
UNIT = 256
TILE = 256
AHEAD = 2


def rows_at(index, size):
    return pl.ds(pl.multiple_of(index * size, size), size)


def dot_t(left, right):
    return lax.dot_general(left, right, (((1,), (1,)), ((), ())), preferred_element_type=jnp.float32)


def kernel(
    sizes, text_ref, image_ref, pair_ref, exponent_ref, offset_ref, total,
    raw, pairs, unit, near, far, load_sem, pair_sem, send_sem, near_sem, pass_sem, far_sem,
):
    ring, inner, rows = sizes
    subs = rows // SUB
    units = 2 * (rows // UNIT)
    parts = UNIT // SUB
    me = lax.axis_index("grp") * inner + lax.axis_index("dp")
    odd = lax.rem(me, 2)
    partner = me + 1 - 2 * odd
    onward = lax.rem(me + 2 - 4 * odd + ring, ring)
    behind = lax.rem(me - 2 + 4 * odd + ring, ring)
    sources = (text_ref, image_ref)

    def place(index):
        return (index // inner, lax.rem(index, inner))

    def load(kind, j):
        return pltpu.make_async_copy(
            sources[kind].at[rows_at(j, UNIT)], raw.at[kind, rows_at(j, UNIT)], load_sem.at[kind, j]
        )

    for j in range(rows // UNIT):
        for kind in range(2):
            load(kind, j).start()
    load_pairs = pltpu.make_async_copy(pair_ref, pairs, pair_sem)
    load_pairs.start()

    barrier = pltpu.get_barrier_semaphore()
    for other in (partner, onward, behind):
        pl.semaphore_signal(barrier, inc=1, device_id=place(other), device_id_type=pl.DeviceIdType.MESH)
    pl.semaphore_wait(barrier, 3)

    def own_copy(kind, s):
        return pltpu.make_async_remote_copy(
            src_ref=unit.at[kind, rows_at(s, SUB)],
            dst_ref=near.at[kind, rows_at(s, SUB)],
            send_sem=send_sem.at[kind, s],
            recv_sem=near_sem.at[kind, s],
            device_id=place(partner),
            device_id_type=pl.DeviceIdType.MESH,
        )

    def pass_copy(kind, s):
        return pltpu.make_async_remote_copy(
            src_ref=near.at[kind, rows_at(s, SUB)],
            dst_ref=far.at[kind, rows_at(s, SUB)],
            send_sem=pass_sem.at[kind, s],
            recv_sem=far_sem.at[kind, s],
            device_id=place(onward),
            device_id_type=pl.DeviceIdType.MESH,
        )

    @pl.loop(0, rows // UNIT)
    def _(j):
        for kind in range(2):
            load(kind, j).wait()
            for part in range(parts):
                s = j * parts + part
                at = rows_at(s, SUB)
                values = raw[kind, at, :].astype(jnp.float32)
                inverse = lax.rsqrt(jnp.sum(values * values, -1, keepdims=True) + 1e-06)
                unit[kind, at, :] = (values * inverse).astype(jnp.bfloat16)

                @pl.when(j * 2 + kind < AHEAD)
                def _():
                    own_copy(kind, s).start()

    load_pairs.wait()
    top = jnp.exp(jnp.full((1, UNIT), exponent_ref[0], jnp.float32))
    scale = top * -LOG2E
    shift = jnp.full((1, UNIT), offset_ref[0], jnp.float32) * -LOG2E

    def spread(kind, block):
        for r in range(rows // TILE):
            at = pl.ds(r * TILE, TILE)
            power = scale * dot_t(unit[1 - kind, at, :], block) + shift
            panel = (top / (1.0 + jnp.exp2(power))).astype(jnp.bfloat16)
            total[1 - kind, at, :] += jnp.dot(panel, block, preferred_element_type=jnp.float32)

    def own_block(j):
        block_at = rows_at(j, UNIT)
        block = unit[1, block_at, :]
        match = pairs[:, block_at]
        for r in range(rows // TILE):
            at = pl.ds(r * TILE, TILE)
            captions = unit[0, at, :]
            hit = match == lax.broadcasted_iota(jnp.int32, (TILE, UNIT), 0) + r * TILE
            power = scale * dot_t(captions, block) + shift
            panel = top / (1.0 + jnp.exp2(jnp.where(hit, -power, power)))
            panel = jnp.where(hit, -panel, panel).astype(jnp.bfloat16)
            text_term = jnp.dot(panel, block, preferred_element_type=jnp.float32)
            image_term = lax.dot_general(
                panel, captions, (((0,), (0,)), ((), ())), preferred_element_type=jnp.float32
            )

            @pl.when(j == 0)
            def _():
                total[0, at, :] = text_term

            @pl.when(j > 0)
            def _():
                total[0, at, :] += text_term

            if r == 0:
                total[1, block_at, :] = image_term
            else:
                total[1, block_at, :] += image_term

    @pl.loop(0, rows // UNIT)
    def _(j):
        own_block(j)

    @pl.loop(0, units + 1)
    def _(u):
        @pl.when(u < units)
        def _():
            kind, j = lax.rem(u, 2), u // 2
            for part in range(parts):
                s = j * parts + part
                own_copy(kind, s).wait_recv()
                pass_copy(kind, s).start()

                @pl.when(u + AHEAD < units)
                def _():
                    later = u + AHEAD
                    own_copy(lax.rem(later, 2), (later // 2) * parts + part).start()

            spread(kind, near[kind, rows_at(j, UNIT), :])

        @pl.when(u > 0)
        def _():
            kind, j = lax.rem(u - 1, 2), (u - 1) // 2
            for part in range(parts):
                pass_copy(kind, j * parts + part).wait_recv()
            spread(kind, far[kind, rows_at(j, UNIT), :])

    @pl.loop(0, subs)
    def _(s):
        for kind in range(2):
            own_copy(kind, s).wait_send()
            pass_copy(kind, s).wait_send()


def backward_kernel(total, text_ref, image_ref, text_out, image_out):
    for kind, (ref, out) in enumerate(((text_ref, text_out), (image_ref, image_out))):
        values = ref[...].astype(jnp.float32)
        inverse = lax.rsqrt(jnp.sum(values * values, -1, keepdims=True) + 1e-06)
        values = values * inverse
        grad = total[kind]
        out[...] = inverse * (grad - values * jnp.sum(values * grad, -1, keepdims=True))


def local(ring, inner, photo, sentence, companion, exponent, offset):
    rows, width = photo.shape
    subs = rows // SUB
    anywhere = pl.BlockSpec(memory_space=pltpu.HBM)
    vmem = pl.BlockSpec(memory_space=pltpu.VMEM)
    smem = pl.BlockSpec(memory_space=pltpu.SMEM)
    blocks = pltpu.VMEM((2, rows, width), jnp.bfloat16)
    total = pl.pallas_call(
        functools.partial(kernel, (ring, inner, rows)),
        out_shape=jax.ShapeDtypeStruct((2, rows, width), jnp.float32),
        in_specs=[anywhere, anywhere, anywhere, smem, smem],
        out_specs=vmem,
        scratch_shapes=[
            blocks,
            pltpu.VMEM((1, rows), jnp.int32),
            blocks,
            blocks,
            blocks,
            pltpu.SemaphoreType.DMA((2, rows // UNIT)),
            pltpu.SemaphoreType.DMA,
            pltpu.SemaphoreType.DMA((2, subs)),
            pltpu.SemaphoreType.DMA((2, subs)),
            pltpu.SemaphoreType.DMA((2, subs)),
            pltpu.SemaphoreType.DMA((2, subs)),
        ],
        compiler_params=pltpu.CompilerParams(
            collective_id=0, has_side_effects=True, vmem_limit_bytes=40 * 1024 * 1024
        ),
        cost_estimate=pl.CostEstimate(
            flops=22 * rows * rows * width, bytes_accessed=12 * rows * width, transcendentals=10 * rows * rows
        ),
    )(sentence, photo, companion, exponent, offset)
    tile = 256
    row_block = pl.BlockSpec((tile, width), lambda i: (i, 0))
    grad = jax.ShapeDtypeStruct((rows, width), jnp.float32)
    text_grad, image_grad = pl.pallas_call(
        backward_kernel,
        grid=(rows // tile,),
        out_shape=(grad, grad),
        in_specs=[pl.BlockSpec((2, tile, width), lambda i: (0, i, 0)), row_block, row_block],
        out_specs=(row_block, row_block),
        compiler_params=pltpu.CompilerParams(vmem_limit_bytes=24 * 1024 * 1024),
        cost_estimate=pl.CostEstimate(
            flops=20 * rows * width, bytes_accessed=20 * rows * width, transcendentals=0
        ),
    )(total, sentence, photo)
    return image_grad, text_grad


def solution(mesh):
    inner = mesh.shape["dp"]
    ring = mesh.shape["grp"] * inner
    placed = (P(("grp", "dp"), None), P(("grp", "dp"), None), P(("grp", "dp"), None), P(), P())
    return jax.shard_map(
        functools.partial(local, ring, inner),
        mesh=mesh,
        in_specs=placed,
        out_specs=(P(("grp", "dp"), None), P(("grp", "dp"), None)),
        check_vma=False,
    )
```

```python
import functools

import jax
import jax.numpy as jnp
from jax import lax
from jax.experimental import pallas as pl
from jax.experimental.pallas import tpu as pltpu
from jax.sharding import PartitionSpec as P

LOG2E = 1.4426950408889634
SUB = 128
UNIT = 256
TILE = 256
AHEAD = 6
LAG = 4


def rows_at(index, size):
    return pl.ds(pl.multiple_of(index * size, size), size)


def dot_t(left, right):
    return lax.dot_general(left, right, (((1,), (1,)), ((), ())), preferred_element_type=jnp.float32)


def kernel(
    sizes, text_ref, image_ref, pair_ref, exponent_ref, offset_ref, total,
    raw, pairs, unit, near, far, load_sem, pair_sem, send_sem, near_sem, pass_sem, far_sem,
):
    ring, inner, rows = sizes
    subs = rows // SUB
    parts = UNIT // SUB
    me = lax.axis_index("grp") * inner + lax.axis_index("dp")
    odd = lax.rem(me, 2)
    partner = me + 1 - 2 * odd
    onward = lax.rem(me + 2 - 4 * odd + ring, ring)
    behind = lax.rem(me - 2 + 4 * odd + ring, ring)
    sources = (text_ref, image_ref)

    def place(index):
        return (index // inner, lax.rem(index, inner))

    def load(kind, j):
        return pltpu.make_async_copy(
            sources[kind].at[rows_at(j, UNIT)], raw.at[kind, rows_at(j, UNIT)], load_sem.at[kind, j]
        )

    for j in range(rows // UNIT):
        for kind in range(2):
            load(kind, j).start()
    load_pairs = pltpu.make_async_copy(pair_ref, pairs, pair_sem)
    load_pairs.start()

    barrier = pltpu.get_barrier_semaphore()
    for other in (partner, onward, behind):
        pl.semaphore_signal(barrier, inc=1, device_id=place(other), device_id_type=pl.DeviceIdType.MESH)
    pl.semaphore_wait(barrier, 3)

    def own_copy(kind, s):
        return pltpu.make_async_remote_copy(
            src_ref=unit.at[kind, rows_at(s, SUB)],
            dst_ref=near.at[kind, rows_at(s, SUB)],
            send_sem=send_sem.at[kind, s],
            recv_sem=near_sem.at[kind, s],
            device_id=place(partner),
            device_id_type=pl.DeviceIdType.MESH,
        )

    def pass_copy(kind, s):
        return pltpu.make_async_remote_copy(
            src_ref=near.at[kind, rows_at(s, SUB)],
            dst_ref=far.at[kind, rows_at(s, SUB)],
            send_sem=pass_sem.at[kind, s],
            recv_sem=far_sem.at[kind, s],
            device_id=place(onward),
            device_id_type=pl.DeviceIdType.MESH,
        )

    @pl.loop(0, rows // UNIT)
    def _(j):
        for kind in range(2):
            load(kind, j).wait()
            for part in range(parts):
                s = j * parts + part
                at = rows_at(s, SUB)
                values = raw[kind, at, :].astype(jnp.float32)
                inverse = lax.rsqrt(jnp.sum(values * values, -1, keepdims=True) + 1e-06)
                unit[kind, at, :] = (values * inverse).astype(jnp.bfloat16)
                total[kind, at, :] = jnp.zeros_like(values)

                @pl.when((j * 2 + kind) * parts + part < AHEAD)
                def _():
                    own_copy(kind, s).start()

    load_pairs.wait()
    top = jnp.exp(jnp.full((1, UNIT), exponent_ref[0], jnp.float32))
    scale = top * -LOG2E
    shift = jnp.full((1, UNIT), offset_ref[0], jnp.float32) * -LOG2E

    def spread(kind, block):
        for r in range(rows // TILE):
            at = pl.ds(r * TILE, TILE)
            power = scale * dot_t(unit[1 - kind, at, :], block) + shift
            panel = (top / (1.0 + jnp.exp2(power))).astype(jnp.bfloat16)
            total[1 - kind, at, :] += jnp.dot(panel, block, preferred_element_type=jnp.float32)

    def own_block(j):
        block_at = rows_at(j, UNIT)
        block = unit[1, block_at, :]
        match = pairs[:, block_at]
        for r in range(rows // TILE):
            at = pl.ds(r * TILE, TILE)
            captions = unit[0, at, :]
            hit = match == lax.broadcasted_iota(jnp.int32, (TILE, UNIT), 0) + r * TILE
            power = scale * dot_t(captions, block) + shift
            panel = top / (1.0 + jnp.exp2(jnp.where(hit, -power, power)))
            panel = jnp.where(hit, -panel, panel).astype(jnp.bfloat16)
            text_term = jnp.dot(panel, block, preferred_element_type=jnp.float32)
            image_term = lax.dot_general(
                panel, captions, (((0,), (0,)), ((), ())), preferred_element_type=jnp.float32
            )

            total[0, at, :] += text_term
            total[1, block_at, :] += image_term

    def place_of(v):
        return lax.rem(v // parts, 2), (v // (2 * parts)) * parts + lax.rem(v, parts)

    own_block(0)

    @pl.loop(0, 2 * subs + LAG - 1)
    def _(v):
        @pl.when(v < 2 * subs)
        def _():
            kind, s = place_of(v)
            own_copy(kind, s).wait_recv()
            pass_copy(kind, s).start()

            @pl.when(v + AHEAD < 2 * subs)
            def _():
                own_copy(*place_of(v + AHEAD)).start()

        u = v // parts

        @pl.when(lax.rem(v, parts) == 0)
        def _():
            @pl.when(u + 1 < rows // UNIT)
            def _():
                own_block(u + 1)

            @pl.when(v >= LAG)
            def _():
                w = u - LAG // parts
                kind, j = lax.rem(w, 2), w // 2
                for part in range(parts):
                    pass_copy(kind, j * parts + part).wait_recv()
                spread(kind, far[kind, rows_at(j, UNIT), :])

        @pl.when((lax.rem(v, parts) == parts - 1) & (v < 2 * subs))
        def _():
            kind, j = lax.rem(u, 2), u // 2
            spread(kind, near[kind, rows_at(j, UNIT), :])

    @pl.loop(0, subs)
    def _(s):
        for kind in range(2):
            own_copy(kind, s).wait_send()
            pass_copy(kind, s).wait_send()


def backward_kernel(total, text_ref, image_ref, text_out, image_out):
    for kind, (ref, out) in enumerate(((text_ref, text_out), (image_ref, image_out))):
        values = ref[...].astype(jnp.float32)
        inverse = lax.rsqrt(jnp.sum(values * values, -1, keepdims=True) + 1e-06)
        values = values * inverse
        grad = total[kind]
        out[...] = inverse * (grad - values * jnp.sum(values * grad, -1, keepdims=True))


def local(ring, inner, photo, sentence, companion, exponent, offset):
    rows, width = photo.shape
    subs = rows // SUB
    anywhere = pl.BlockSpec(memory_space=pltpu.HBM)
    vmem = pl.BlockSpec(memory_space=pltpu.VMEM)
    smem = pl.BlockSpec(memory_space=pltpu.SMEM)
    blocks = pltpu.VMEM((2, rows, width), jnp.bfloat16)
    total = pl.pallas_call(
        functools.partial(kernel, (ring, inner, rows)),
        out_shape=jax.ShapeDtypeStruct((2, rows, width), jnp.float32),
        in_specs=[anywhere, anywhere, anywhere, smem, smem],
        out_specs=vmem,
        scratch_shapes=[
            blocks,
            pltpu.VMEM((1, rows), jnp.int32),
            blocks,
            blocks,
            blocks,
            pltpu.SemaphoreType.DMA((2, rows // UNIT)),
            pltpu.SemaphoreType.DMA,
            pltpu.SemaphoreType.DMA((2, subs)),
            pltpu.SemaphoreType.DMA((2, subs)),
            pltpu.SemaphoreType.DMA((2, subs)),
            pltpu.SemaphoreType.DMA((2, subs)),
        ],
        compiler_params=pltpu.CompilerParams(
            collective_id=0, has_side_effects=True, vmem_limit_bytes=40 * 1024 * 1024
        ),
        cost_estimate=pl.CostEstimate(
            flops=22 * rows * rows * width, bytes_accessed=12 * rows * width, transcendentals=10 * rows * rows
        ),
    )(sentence, photo, companion, exponent, offset)
    tile = 256
    row_block = pl.BlockSpec((tile, width), lambda i: (i, 0))
    grad = jax.ShapeDtypeStruct((rows, width), jnp.float32)
    text_grad, image_grad = pl.pallas_call(
        backward_kernel,
        grid=(rows // tile,),
        out_shape=(grad, grad),
        in_specs=[pl.BlockSpec((2, tile, width), lambda i: (0, i, 0)), row_block, row_block],
        out_specs=(row_block, row_block),
        compiler_params=pltpu.CompilerParams(vmem_limit_bytes=24 * 1024 * 1024),
        cost_estimate=pl.CostEstimate(
            flops=20 * rows * width, bytes_accessed=20 * rows * width, transcendentals=0
        ),
    )(total, sentence, photo)
    return image_grad, text_grad


def solution(mesh):
    inner = mesh.shape["dp"]
    ring = mesh.shape["grp"] * inner
    placed = (P(("grp", "dp"), None), P(("grp", "dp"), None), P(("grp", "dp"), None), P(), P())
    return jax.shard_map(
        functools.partial(local, ring, inner),
        mesh=mesh,
        in_specs=placed,
        out_specs=(P(("grp", "dp"), None), P(("grp", "dp"), None)),
        check_vma=False,
    )
```

```python
import functools

import jax
import jax.numpy as jnp
from jax import lax
from jax.experimental import pallas as pl
from jax.experimental.pallas import tpu as pltpu
from jax.sharding import PartitionSpec as P

LOG2E = 1.4426950408889634
SUB = 64
UNIT = 256
TILE = 256
AHEAD = 12
LAG = 6


def rows_at(index, size):
    return pl.ds(pl.multiple_of(index * size, size), size)


def dot_t(left, right):
    return lax.dot_general(left, right, (((1,), (1,)), ((), ())), preferred_element_type=jnp.float32)


def kernel(
    sizes, text_ref, image_ref, pair_ref, exponent_ref, offset_ref, total,
    raw, pairs, norm, unit, near, far, load_sem, pair_sem, send_sem, near_sem, pass_sem, far_sem,
):
    ring, inner, rows = sizes
    subs = rows // SUB
    parts = UNIT // SUB
    me = lax.axis_index("grp") * inner + lax.axis_index("dp")
    odd = lax.rem(me, 2)
    partner = me + 1 - 2 * odd
    onward = lax.rem(me + 2 - 4 * odd + ring, ring)
    behind = lax.rem(me - 2 + 4 * odd + ring, ring)
    sources = (text_ref, image_ref)

    def place(index):
        return (index // inner, lax.rem(index, inner))

    def load(kind, j):
        return pltpu.make_async_copy(
            sources[kind].at[rows_at(j, UNIT)], raw.at[kind, rows_at(j, UNIT)], load_sem.at[kind, j]
        )

    for j in range(rows // UNIT):
        for kind in range(2):
            load(kind, j).start()
    load_pairs = pltpu.make_async_copy(pair_ref, pairs, pair_sem)
    load_pairs.start()

    barrier = pltpu.get_barrier_semaphore()
    for other in (partner, onward, behind):
        pl.semaphore_signal(barrier, inc=1, device_id=place(other), device_id_type=pl.DeviceIdType.MESH)
    pl.semaphore_wait(barrier, 3)

    def own_copy(kind, s):
        return pltpu.make_async_remote_copy(
            src_ref=unit.at[kind, rows_at(s, SUB)],
            dst_ref=near.at[kind, rows_at(s, SUB)],
            send_sem=send_sem.at[kind, s],
            recv_sem=near_sem.at[kind, s],
            device_id=place(partner),
            device_id_type=pl.DeviceIdType.MESH,
        )

    def pass_copy(kind, s):
        return pltpu.make_async_remote_copy(
            src_ref=near.at[kind, rows_at(s, SUB)],
            dst_ref=far.at[kind, rows_at(s, SUB)],
            send_sem=pass_sem.at[kind, s],
            recv_sem=far_sem.at[kind, s],
            device_id=place(onward),
            device_id_type=pl.DeviceIdType.MESH,
        )

    @pl.loop(0, rows // UNIT)
    def _(j):
        for kind in range(2):
            load(kind, j).wait()
            for part in range(parts):
                s = j * parts + part
                at = rows_at(s, SUB)
                values = raw[kind, at, :].astype(jnp.float32)
                inverse = lax.rsqrt(jnp.sum(values * values, -1, keepdims=True) + 1e-06)
                norm[kind, at, :] = inverse
                unit[kind, at, :] = (values * inverse).astype(jnp.bfloat16)
                total[kind, at, :] = jnp.zeros_like(values)

                @pl.when((j * 2 + kind) * parts + part < AHEAD)
                def _():
                    own_copy(kind, s).start()

    load_pairs.wait()
    top = jnp.exp(jnp.full((1, UNIT), exponent_ref[0], jnp.float32))
    scale = top * -LOG2E
    shift = jnp.full((1, UNIT), offset_ref[0], jnp.float32) * -LOG2E

    def spread(kind, block):
        for r in range(rows // TILE):
            at = pl.ds(r * TILE, TILE)
            power = scale * dot_t(unit[1 - kind, at, :], block) + shift
            panel = (top / (1.0 + jnp.exp2(power))).astype(jnp.bfloat16)
            total[1 - kind, at, :] += jnp.dot(panel, block, preferred_element_type=jnp.float32)

    def own_block(j):
        block_at = rows_at(j, UNIT)
        block = unit[1, block_at, :]
        match = pairs[:, block_at]
        for r in range(rows // TILE):
            at = pl.ds(r * TILE, TILE)
            captions = unit[0, at, :]
            hit = match == lax.broadcasted_iota(jnp.int32, (TILE, UNIT), 0) + r * TILE
            power = scale * dot_t(captions, block) + shift
            panel = top / (1.0 + jnp.exp2(jnp.where(hit, -power, power)))
            panel = jnp.where(hit, -panel, panel).astype(jnp.bfloat16)
            text_term = jnp.dot(panel, block, preferred_element_type=jnp.float32)
            image_term = lax.dot_general(
                panel, captions, (((0,), (0,)), ((), ())), preferred_element_type=jnp.float32
            )

            total[0, at, :] += text_term
            total[1, block_at, :] += image_term

    def place_of(v):
        return lax.rem(v // parts, 2), (v // (2 * parts)) * parts + lax.rem(v, parts)

    own_block(0)

    def spread_far(w):
        kind, j = lax.rem(w, 2), w // 2
        for part in range(parts):
            pass_copy(kind, j * parts + part).wait_recv()
        spread(kind, far[kind, rows_at(j, UNIT), :])

    def finish(kind):
        @pl.loop(0, rows // UNIT)
        def _(j):
            at = rows_at(j, UNIT)
            inverse = norm[kind, at, :]
            values = raw[kind, at, :].astype(jnp.float32) * inverse
            grad = total[kind, at, :]
            total[kind, at, :] = inverse * (grad - values * jnp.sum(values * grad, -1, keepdims=True))

    @pl.loop(0, 2 * subs + parts)
    def _(v):
        u = v // parts

        @pl.when(v < 2 * subs)
        def _():
            kind, s = place_of(v)
            own_copy(kind, s).wait_recv()
            pass_copy(kind, s).start()

            @pl.when(v + AHEAD < 2 * subs)
            def _():
                own_copy(*place_of(v + AHEAD)).start()

            @pl.when((lax.rem(v, parts) == 0) & (u + 1 < rows // UNIT))
            def _():
                own_block(u + 1)

            @pl.when(lax.rem(v, parts) == parts - 1)
            def _():
                near_kind, j = lax.rem(u, 2), u // 2
                spread(near_kind, near[near_kind, rows_at(j, UNIT), :])

        @pl.when(v == 2 * subs)
        def _():
            finish(1)

        @pl.when((v >= LAG) & (lax.rem(v, parts) == LAG % parts))
        def _():
            spread_far((v - LAG) // parts)

    finish(0)

    @pl.loop(0, subs)
    def _(s):
        for kind in range(2):
            own_copy(kind, s).wait_send()
            pass_copy(kind, s).wait_send()


def move_kernel(total, text_out, image_out, sems):
    rows = total.shape[1]
    copies = [
        pltpu.make_async_copy(
            total.at[kind, pl.ds(j * UNIT, UNIT)], out.at[pl.ds(j * UNIT, UNIT)], sems.at[kind, j]
        )
        for kind, out in enumerate((text_out, image_out))
        for j in range(rows // UNIT)
    ]
    for copy in copies:
        copy.start()
    for copy in copies:
        copy.wait()


def local(ring, inner, photo, sentence, companion, exponent, offset):
    rows, width = photo.shape
    subs = rows // SUB
    anywhere = pl.BlockSpec(memory_space=pl.ANY)
    vmem = pl.BlockSpec(memory_space=pltpu.VMEM)
    smem = pl.BlockSpec(memory_space=pltpu.SMEM)
    blocks = pltpu.VMEM((2, rows, width), jnp.bfloat16)
    total = pl.pallas_call(
        functools.partial(kernel, (ring, inner, rows)),
        out_shape=jax.ShapeDtypeStruct((2, rows, width), jnp.float32),
        in_specs=[anywhere, anywhere, anywhere, smem, smem],
        out_specs=vmem,
        scratch_shapes=[
            blocks,
            pltpu.VMEM((1, rows), jnp.int32),
            pltpu.VMEM((2, rows, 1), jnp.float32),
            blocks,
            blocks,
            blocks,
            pltpu.SemaphoreType.DMA((2, rows // UNIT)),
            pltpu.SemaphoreType.DMA,
            pltpu.SemaphoreType.DMA((2, subs)),
            pltpu.SemaphoreType.DMA((2, subs)),
            pltpu.SemaphoreType.DMA((2, subs)),
            pltpu.SemaphoreType.DMA((2, subs)),
        ],
        compiler_params=pltpu.CompilerParams(
            collective_id=0, has_side_effects=True, vmem_limit_bytes=40 * 1024 * 1024
        ),
        cost_estimate=pl.CostEstimate(
            flops=22 * rows * rows * width, bytes_accessed=12 * rows * width, transcendentals=10 * rows * rows
        ),
    )(sentence, photo, companion, exponent, offset)
    grad = jax.ShapeDtypeStruct((rows, width), jnp.float32)
    text_grad, image_grad = pl.pallas_call(
        move_kernel,
        out_shape=(grad, grad),
        in_specs=[vmem],
        out_specs=(anywhere, anywhere),
        scratch_shapes=[pltpu.SemaphoreType.DMA((2, rows // UNIT))],
        compiler_params=pltpu.CompilerParams(vmem_limit_bytes=24 * 1024 * 1024),
        cost_estimate=pl.CostEstimate(flops=0, bytes_accessed=16 * rows * width, transcendentals=0),
    )(total)
    return image_grad, text_grad


def solution(mesh):
    inner = mesh.shape["dp"]
    ring = mesh.shape["grp"] * inner
    placed = (P(("grp", "dp"), None), P(("grp", "dp"), None), P(("grp", "dp"), None), P(), P())
    return jax.shard_map(
        functools.partial(local, ring, inner),
        mesh=mesh,
        in_specs=placed,
        out_specs=(P(("grp", "dp"), None), P(("grp", "dp"), None)),
        check_vma=False,
    )
```

```python
import functools

import jax
import jax.numpy as jnp
from jax import lax
from jax.experimental import pallas as pl
from jax.experimental.pallas import tpu as pltpu
from jax.sharding import PartitionSpec as P

SUB = 64
UNIT = 256
TILE = 512
AHEAD = 12
LAG = 6


def rows_at(index, size):
    return pl.ds(pl.multiple_of(index * size, size), size)


def dot_t(left, right):
    return lax.dot_general(left, right, (((1,), (1,)), ((), ())), preferred_element_type=jnp.float32)


def kernel(
    sizes, text_ref, image_ref, pair_ref, exponent_ref, offset_ref, total,
    raw, pairs, norm, unit, near, far, load_sem, pair_sem, send_sem, near_sem, pass_sem, far_sem,
):
    ring, inner, rows = sizes
    subs = rows // SUB
    parts = UNIT // SUB
    me = lax.axis_index("grp") * inner + lax.axis_index("dp")
    odd = lax.rem(me, 2)
    partner = me + 1 - 2 * odd
    onward = lax.rem(me + 2 - 4 * odd + ring, ring)
    behind = lax.rem(me - 2 + 4 * odd + ring, ring)
    sources = (text_ref, image_ref)

    def place(index):
        return (index // inner, lax.rem(index, inner))

    def load(kind, j):
        return pltpu.make_async_copy(
            sources[kind].at[rows_at(j, UNIT)], raw.at[kind, rows_at(j, UNIT)], load_sem.at[kind, j]
        )

    for j in range(rows // UNIT):
        for kind in range(2):
            load(kind, j).start()
    load_pairs = pltpu.make_async_copy(pair_ref, pairs, pair_sem)
    load_pairs.start()

    barrier = pltpu.get_barrier_semaphore()
    for other in (partner, onward, behind):
        pl.semaphore_signal(barrier, inc=1, device_id=place(other), device_id_type=pl.DeviceIdType.MESH)
    pl.semaphore_wait(barrier, 3)

    def own_copy(kind, s):
        return pltpu.make_async_remote_copy(
            src_ref=unit.at[kind, rows_at(s, SUB)],
            dst_ref=near.at[kind, rows_at(s, SUB)],
            send_sem=send_sem.at[kind, s],
            recv_sem=near_sem.at[kind, s],
            device_id=place(partner),
            device_id_type=pl.DeviceIdType.MESH,
        )

    def pass_copy(kind, s):
        return pltpu.make_async_remote_copy(
            src_ref=near.at[kind, rows_at(s, SUB)],
            dst_ref=far.at[kind, rows_at(s, SUB)],
            send_sem=pass_sem.at[kind, s],
            recv_sem=far_sem.at[kind, s],
            device_id=place(onward),
            device_id_type=pl.DeviceIdType.MESH,
        )

    @pl.loop(0, rows // UNIT)
    def _(j):
        for kind in range(2):
            load(kind, j).wait()
            for part in range(parts):
                s = j * parts + part
                at = rows_at(s, SUB)
                values = raw[kind, at, :].astype(jnp.float32)
                inverse = lax.rsqrt(jnp.sum(values * values, -1, keepdims=True) + 1e-06)
                norm[kind, at, :] = inverse
                unit[kind, at, :] = (values * inverse).astype(jnp.bfloat16)
                total[kind, at, :] = jnp.zeros_like(values)

                @pl.when((j * 2 + kind) * parts + part < AHEAD)
                def _():
                    own_copy(kind, s).start()

    load_pairs.wait()
    half = 0.5 * jnp.exp(jnp.full((1, UNIT), exponent_ref[0], jnp.float32))
    shift = jnp.full((1, UNIT), 0.5 * offset_ref[0], jnp.float32)

    def spread(kind, block):
        for r in range(rows // TILE):
            at = pl.ds(r * TILE, TILE)
            slope = jnp.tanh(half * dot_t(unit[1 - kind, at, :], block) + shift)
            panel = (half + half * slope).astype(jnp.bfloat16)
            total[1 - kind, at, :] += jnp.dot(panel, block, preferred_element_type=jnp.float32)

    def own_block(j):
        block_at = rows_at(j, UNIT)
        block = unit[1, block_at, :]
        match = pairs[:, block_at]
        for r in range(rows // TILE):
            at = pl.ds(r * TILE, TILE)
            captions = unit[0, at, :]
            hit = match == lax.broadcasted_iota(jnp.int32, (TILE, UNIT), 0) + r * TILE
            slope = jnp.tanh(half * dot_t(captions, block) + shift)
            panel = (half * slope + jnp.where(hit, -half, half)).astype(jnp.bfloat16)
            text_term = jnp.dot(panel, block, preferred_element_type=jnp.float32)
            image_term = lax.dot_general(
                panel, captions, (((0,), (0,)), ((), ())), preferred_element_type=jnp.float32
            )

            total[0, at, :] += text_term
            total[1, block_at, :] += image_term

    def place_of(v):
        return lax.rem(v // parts, 2), (v // (2 * parts)) * parts + lax.rem(v, parts)

    own_block(0)

    def spread_far(w):
        kind, j = lax.rem(w, 2), w // 2
        for part in range(parts):
            pass_copy(kind, j * parts + part).wait_recv()
        spread(kind, far[kind, rows_at(j, UNIT), :])

    def finish(kind):
        @pl.loop(0, rows // UNIT)
        def _(j):
            at = rows_at(j, UNIT)
            inverse = norm[kind, at, :]
            values = raw[kind, at, :].astype(jnp.float32) * inverse
            grad = total[kind, at, :]
            total[kind, at, :] = inverse * (grad - values * jnp.sum(values * grad, -1, keepdims=True))

    @pl.loop(0, 2 * subs + parts)
    def _(v):
        u = v // parts

        @pl.when(v < 2 * subs)
        def _():
            kind, s = place_of(v)
            own_copy(kind, s).wait_recv()
            pass_copy(kind, s).start()

            @pl.when(v + AHEAD < 2 * subs)
            def _():
                own_copy(*place_of(v + AHEAD)).start()

            @pl.when((lax.rem(v, parts) == 0) & (u + 1 < rows // UNIT))
            def _():
                own_block(u + 1)

            @pl.when(lax.rem(v, parts) == parts - 1)
            def _():
                near_kind, j = lax.rem(u, 2), u // 2
                spread(near_kind, near[near_kind, rows_at(j, UNIT), :])

        @pl.when(v == 2 * subs)
        def _():
            finish(1)

        @pl.when((v >= LAG) & (lax.rem(v, parts) == LAG % parts))
        def _():
            spread_far((v - LAG) // parts)

    finish(0)

    @pl.loop(0, subs)
    def _(s):
        for kind in range(2):
            own_copy(kind, s).wait_send()
            pass_copy(kind, s).wait_send()


def move_kernel(total, text_out, image_out, sems):
    rows = total.shape[1]
    copies = [
        pltpu.make_async_copy(
            total.at[kind, pl.ds(j * UNIT, UNIT)], out.at[pl.ds(j * UNIT, UNIT)], sems.at[kind, j]
        )
        for kind, out in enumerate((text_out, image_out))
        for j in range(rows // UNIT)
    ]
    for copy in copies:
        copy.start()
    for copy in copies:
        copy.wait()


def local(ring, inner, photo, sentence, companion, exponent, offset):
    rows, width = photo.shape
    subs = rows // SUB
    anywhere = pl.BlockSpec(memory_space=pl.ANY)
    vmem = pl.BlockSpec(memory_space=pltpu.VMEM)
    smem = pl.BlockSpec(memory_space=pltpu.SMEM)
    blocks = pltpu.VMEM((2, rows, width), jnp.bfloat16)
    total = pl.pallas_call(
        functools.partial(kernel, (ring, inner, rows)),
        out_shape=jax.ShapeDtypeStruct((2, rows, width), jnp.float32),
        in_specs=[anywhere, anywhere, anywhere, smem, smem],
        out_specs=vmem,
        scratch_shapes=[
            blocks,
            pltpu.VMEM((1, rows), jnp.int32),
            pltpu.VMEM((2, rows, 1), jnp.float32),
            blocks,
            blocks,
            blocks,
            pltpu.SemaphoreType.DMA((2, rows // UNIT)),
            pltpu.SemaphoreType.DMA,
            pltpu.SemaphoreType.DMA((2, subs)),
            pltpu.SemaphoreType.DMA((2, subs)),
            pltpu.SemaphoreType.DMA((2, subs)),
            pltpu.SemaphoreType.DMA((2, subs)),
        ],
        compiler_params=pltpu.CompilerParams(
            collective_id=0, has_side_effects=True, vmem_limit_bytes=40 * 1024 * 1024
        ),
        cost_estimate=pl.CostEstimate(
            flops=22 * rows * rows * width, bytes_accessed=12 * rows * width, transcendentals=10 * rows * rows
        ),
    )(sentence, photo, companion, exponent, offset)
    grad = jax.ShapeDtypeStruct((rows, width), jnp.float32)
    text_grad, image_grad = pl.pallas_call(
        move_kernel,
        out_shape=(grad, grad),
        in_specs=[vmem],
        out_specs=(anywhere, anywhere),
        scratch_shapes=[pltpu.SemaphoreType.DMA((2, rows // UNIT))],
        compiler_params=pltpu.CompilerParams(vmem_limit_bytes=24 * 1024 * 1024),
        cost_estimate=pl.CostEstimate(flops=0, bytes_accessed=16 * rows * width, transcendentals=0),
    )(total)
    return image_grad, text_grad


def solution(mesh):
    inner = mesh.shape["dp"]
    ring = mesh.shape["grp"] * inner
    placed = (P(("grp", "dp"), None), P(("grp", "dp"), None), P(("grp", "dp"), None), P(), P())
    return jax.shard_map(
        functools.partial(local, ring, inner),
        mesh=mesh,
        in_specs=placed,
        out_specs=(P(("grp", "dp"), None), P(("grp", "dp"), None)),
        check_vma=False,
    )
```

```python
import functools

import jax
import jax.numpy as jnp
from jax import lax
from jax.experimental import pallas as pl
from jax.experimental.pallas import tpu as pltpu
from jax.sharding import PartitionSpec as P

SUB = 64
UNIT = 256
TILE = 512
AHEAD = 12
LAG = 6


def rows_at(index, size):
    return pl.ds(pl.multiple_of(index * size, size), size)


def dot_t(left, right):
    return lax.dot_general(left, right, (((1,), (1,)), ((), ())), preferred_element_type=jnp.float32)


def kernel(
    sizes, text_ref, image_ref, pair_ref, exponent_ref, offset_ref, total,
    raw, pairs, norm, unit, near, far, load_sem, pair_sem, send_sem, near_sem, pass_sem, far_sem,
):
    ring, inner, rows = sizes
    subs = rows // SUB
    parts = UNIT // SUB
    me = lax.axis_index("grp") * inner + lax.axis_index("dp")
    odd = lax.rem(me, 2)
    partner = me + 1 - 2 * odd
    onward = lax.rem(me + 2 - 4 * odd + ring, ring)
    behind = lax.rem(me - 2 + 4 * odd + ring, ring)
    sources = (text_ref, image_ref)

    def place(index):
        return (index // inner, lax.rem(index, inner))

    def load(kind, j):
        return pltpu.make_async_copy(
            sources[kind].at[rows_at(j, UNIT)], raw.at[kind, rows_at(j, UNIT)], load_sem.at[kind, j]
        )

    for j in range(rows // UNIT):
        for kind in range(2):
            load(kind, j).start()
    load_pairs = pltpu.make_async_copy(pair_ref, pairs, pair_sem)
    load_pairs.start()

    barrier = pltpu.get_barrier_semaphore()
    for other in (partner, onward, behind):
        pl.semaphore_signal(barrier, inc=1, device_id=place(other), device_id_type=pl.DeviceIdType.MESH)
    pl.semaphore_wait(barrier, 3)

    def own_copy(kind, s):
        return pltpu.make_async_remote_copy(
            src_ref=unit.at[kind, rows_at(s, SUB)],
            dst_ref=near.at[kind, rows_at(s, SUB)],
            send_sem=send_sem.at[kind, s],
            recv_sem=near_sem.at[kind, s],
            device_id=place(partner),
            device_id_type=pl.DeviceIdType.MESH,
        )

    def pass_copy(kind, s):
        return pltpu.make_async_remote_copy(
            src_ref=near.at[kind, rows_at(s, SUB)],
            dst_ref=far.at[kind, rows_at(s, SUB)],
            send_sem=pass_sem.at[kind, s],
            recv_sem=far_sem.at[kind, s],
            device_id=place(onward),
            device_id_type=pl.DeviceIdType.MESH,
        )

    @pl.loop(0, rows // UNIT)
    def _(j):
        for kind in range(2):
            load(kind, j).wait()
            for part in range(parts):
                s = j * parts + part
                at = rows_at(s, SUB)
                values = raw[kind, at, :].astype(jnp.float32)
                inverse = lax.rsqrt(jnp.sum(values * values, -1, keepdims=True) + 1e-06)
                norm[kind, at, :] = inverse
                unit[kind, at, :] = (values * inverse).astype(jnp.bfloat16)
                total[kind, at, :] = jnp.zeros_like(values)

                @pl.when((j * 2 + kind) * parts + part < AHEAD)
                def _():
                    own_copy(kind, s).start()

    load_pairs.wait()
    half = 0.5 * jnp.exp(jnp.full((1, UNIT), exponent_ref[0], jnp.float32))
    shift = jnp.full((1, UNIT), 0.5 * offset_ref[0], jnp.float32)

    def spread(kind, block):
        for r in range(rows // TILE):
            at = pl.ds(r * TILE, TILE)
            slope = jnp.tanh(half * dot_t(unit[1 - kind, at, :], block) + shift)
            panel = (half + half * slope).astype(jnp.bfloat16)
            total[1 - kind, at, :] += jnp.dot(panel, block, preferred_element_type=jnp.float32)

    def own_block(j):
        block_at = rows_at(j, UNIT)
        block = unit[1, block_at, :]
        match = pairs[:, block_at]
        for r in range(rows // TILE):
            at = pl.ds(r * TILE, TILE)
            captions = unit[0, at, :]
            hit = match == lax.broadcasted_iota(jnp.int32, (TILE, UNIT), 0) + r * TILE
            slope = jnp.tanh(half * dot_t(captions, block) + shift)
            panel = (half * slope + jnp.where(hit, -half, half)).astype(jnp.bfloat16)
            text_term = jnp.dot(panel, block, preferred_element_type=jnp.float32)
            image_term = lax.dot_general(
                panel, captions, (((0,), (0,)), ((), ())), preferred_element_type=jnp.float32
            )

            total[0, at, :] += text_term
            total[1, block_at, :] += image_term

    def place_of(v):
        return lax.rem(v // parts, 2), (v // (2 * parts)) * parts + lax.rem(v, parts)

    def spread_far(w):
        kind, j = lax.rem(w, 2), w // 2
        for part in range(parts):
            pass_copy(kind, j * parts + part).wait_recv()
        spread(kind, far[kind, rows_at(j, UNIT), :])

    def finish(kind):
        @pl.loop(0, rows // UNIT)
        def _(j):
            at = rows_at(j, UNIT)
            inverse = norm[kind, at, :]
            values = raw[kind, at, :].astype(jnp.float32) * inverse
            grad = total[kind, at, :]
            total[kind, at, :] = inverse * (grad - values * jnp.sum(values * grad, -1, keepdims=True))

    @pl.loop(0, 2 * subs + parts)
    def _(v):
        u = v // parts

        @pl.when(v < 2 * subs)
        def _():
            kind, s = place_of(v)
            own_copy(kind, s).wait_recv()
            pass_copy(kind, s).start()

            @pl.when(v + AHEAD < 2 * subs)
            def _():
                own_copy(*place_of(v + AHEAD)).start()

            @pl.when((lax.rem(v, parts) == 1) & (u < rows // UNIT))
            def _():
                own_block(u)

            @pl.when(lax.rem(v, parts) == parts - 1)
            def _():
                near_kind, j = lax.rem(u, 2), u // 2
                spread(near_kind, near[near_kind, rows_at(j, UNIT), :])

        @pl.when(v == 2 * subs)
        def _():
            finish(1)

        @pl.when((v >= LAG) & (lax.rem(v, parts) == LAG % parts))
        def _():
            spread_far((v - LAG) // parts)

    finish(0)

    @pl.loop(0, subs)
    def _(s):
        for kind in range(2):
            own_copy(kind, s).wait_send()
            pass_copy(kind, s).wait_send()


def move_kernel(total, text_out, image_out, sems):
    rows = total.shape[1]
    copies = [
        pltpu.make_async_copy(
            total.at[kind, pl.ds(j * UNIT, UNIT)], out.at[pl.ds(j * UNIT, UNIT)], sems.at[kind, j]
        )
        for kind, out in enumerate((text_out, image_out))
        for j in range(rows // UNIT)
    ]
    for copy in copies:
        copy.start()
    for copy in copies:
        copy.wait()


def local(ring, inner, photo, sentence, companion, exponent, offset):
    rows, width = photo.shape
    subs = rows // SUB
    anywhere = pl.BlockSpec(memory_space=pl.ANY)
    vmem = pl.BlockSpec(memory_space=pltpu.VMEM)
    smem = pl.BlockSpec(memory_space=pltpu.SMEM)
    blocks = pltpu.VMEM((2, rows, width), jnp.bfloat16)
    total = pl.pallas_call(
        functools.partial(kernel, (ring, inner, rows)),
        out_shape=jax.ShapeDtypeStruct((2, rows, width), jnp.float32),
        in_specs=[anywhere, anywhere, anywhere, smem, smem],
        out_specs=vmem,
        scratch_shapes=[
            blocks,
            pltpu.VMEM((1, rows), jnp.int32),
            pltpu.VMEM((2, rows, 1), jnp.float32),
            blocks,
            blocks,
            blocks,
            pltpu.SemaphoreType.DMA((2, rows // UNIT)),
            pltpu.SemaphoreType.DMA,
            pltpu.SemaphoreType.DMA((2, subs)),
            pltpu.SemaphoreType.DMA((2, subs)),
            pltpu.SemaphoreType.DMA((2, subs)),
            pltpu.SemaphoreType.DMA((2, subs)),
        ],
        compiler_params=pltpu.CompilerParams(
            collective_id=0, has_side_effects=True, vmem_limit_bytes=40 * 1024 * 1024
        ),
        cost_estimate=pl.CostEstimate(
            flops=22 * rows * rows * width, bytes_accessed=12 * rows * width, transcendentals=10 * rows * rows
        ),
    )(
        pltpu.with_memory_space_constraint(sentence, pltpu.HBM),
        pltpu.with_memory_space_constraint(photo, pltpu.HBM),
        pltpu.with_memory_space_constraint(companion, pltpu.HBM),
        exponent,
        offset,
    )
    grad = jax.ShapeDtypeStruct((rows, width), jnp.float32)
    text_grad, image_grad = pl.pallas_call(
        move_kernel,
        out_shape=(grad, grad),
        in_specs=[vmem],
        out_specs=(anywhere, anywhere),
        scratch_shapes=[pltpu.SemaphoreType.DMA((2, rows // UNIT))],
        compiler_params=pltpu.CompilerParams(vmem_limit_bytes=24 * 1024 * 1024),
        cost_estimate=pl.CostEstimate(flops=0, bytes_accessed=16 * rows * width, transcendentals=0),
    )(total)
    return image_grad, text_grad


def solution(mesh):
    inner = mesh.shape["dp"]
    ring = mesh.shape["grp"] * inner
    placed = (P(("grp", "dp"), None), P(("grp", "dp"), None), P(("grp", "dp"), None), P(), P())
    return jax.shard_map(
        functools.partial(local, ring, inner),
        mesh=mesh,
        in_specs=placed,
        out_specs=(P(("grp", "dp"), None), P(("grp", "dp"), None)),
        check_vma=False,
    )
```
